32 devices in a mesh: row: 4 (over x, core), col: 8 (over z, y).
Axes of the slice: x: 2, y: 2, z: 4, core: 2. Of those that a mesh axis runs over, the one named last changes fastest.
Arguments:
- kernel: float32 [8192, 8192], P('row', 'col'), as said below
Outputs:
- schur: float32 [8192, 8192], P('row', 'col')
- panels: float32 [8192, 768], P('row')
Inputs may be any that keep to these rules, and one draw needn't show every extreme that they name: kernel is symmetric and positive definite with smallest eigenvalue of order one.
All inputs are finite; a program needn't handle non-finite values.
Results may differ from the reference program's by a relative error of at most 0.00027.
Values sent between devices are 32-bit elements; how exact they have to be, the bound alone decides.
A program may use at most 128 MiB of HBM per device.

```python
import jax
import jax.numpy as jnp
from jax import lax

BLOCK = 256
RB = 8
STEPS = 3
CB = 4
NT = 8192
N_ROW = 4
N_COL = 8


def draw_kernel(key, part):
    direction_key = jax.random.fold_in(key, 21)
    shell_key = jax.random.fold_in(key, 22)
    noise_key = jax.random.fold_in(key, 23)
    level_key = jax.random.fold_in(key, 24)
    stored = jnp.arange(NT)
    row_part = stored // (RB * BLOCK)
    row_local = stored % (RB * BLOCK) // BLOCK
    row_global = (row_local * N_ROW + row_part) * BLOCK + stored % BLOCK
    col_part = stored // (CB * BLOCK)
    col_local = stored % (CB * BLOCK) // BLOCK
    col_global = (col_local * N_COL + col_part) * BLOCK + stored % BLOCK
    vectors = jax.random.normal(direction_key, (NT, 3), jnp.float32)
    lengths = jnp.sqrt(vectors[:, 0] * vectors[:, 0] + vectors[:, 1] * vectors[:, 1] + vectors[:, 2] * vectors[:, 2])
    unit = vectors / jnp.maximum(lengths, 0.001)[:, None]
    shells = jax.random.uniform(shell_key, (NT,), jnp.float32)
    levels = jax.random.uniform(level_key, (NT,), jnp.float32)
    unit_rows = unit[row_global]
    unit_cols = unit[col_global]
    cosine = unit_rows[:, 0:1] * unit_cols[None, :, 0]
    cosine = cosine + unit_rows[:, 1:2] * unit_cols[None, :, 1]
    cosine = cosine + unit_rows[:, 2:3] * unit_cols[None, :, 2]
    angular = jnp.exp((cosine * cosine - 1.0) / 0.5)
    radial = jnp.exp(-jnp.abs(shells[row_global][:, None] - shells[col_global][None, :]) / 0.3)
    smooth = angular * radial
    raw = jax.random.normal(noise_key, (NT, NT), jnp.float32)
    symmetric = (raw + raw.T) * (0.70710678 * 0.5 * NT ** (-0.5))
    symmetric = jnp.take(symmetric, row_global, axis=0)
    symmetric = jnp.take(symmetric, col_global, axis=1)
    same = row_global[:, None] == col_global[None, :]
    nugget = jnp.where(same, (1.5 + levels[row_global])[:, None], 0.0)
    matrix = smooth + symmetric + nugget
    return matrix.astype(jnp.float32)


def setup_inputs(seed: int = 0) -> dict:
    keys = jax.random.split(jax.random.key(seed), 2)
    kernel = draw_kernel(jax.random.fold_in(keys[1], 71), 0)
    return {"kernel": kernel}


def to_matrix(stored):
    grid = stored.reshape(N_ROW, RB, BLOCK, N_COL, CB, BLOCK)
    return grid.transpose(1, 0, 2, 4, 3, 5).reshape(NT, NT)

def to_stored(matrix):
    grid = matrix.reshape(RB, N_ROW, BLOCK, CB, N_COL, BLOCK)
    return grid.transpose(1, 0, 2, 4, 3, 5).reshape(NT, NT)

def reference(kernel):
    matrix = to_matrix(kernel)
    block_ids = jnp.arange(NT) // BLOCK
    collected = []
    for step in range(STEPS):
        start = step * BLOCK
        factor = jnp.linalg.cholesky(matrix[start:start + BLOCK, start:start + BLOCK])
        solved = jax.scipy.linalg.solve_triangular(factor, matrix[:, start:start + BLOCK].T, lower=True).T
        tiled = jnp.tile(factor, (NT // BLOCK, 1))
        panel = jnp.where((block_ids > step)[:, None], solved, jnp.where((block_ids == step)[:, None], tiled, jnp.float32(0.0)))
        matrix = matrix - jnp.dot(panel, panel.T, precision=lax.Precision.HIGHEST)
        collected.append(panel)
    keep = (block_ids >= STEPS)[:, None] & (block_ids >= STEPS)[None, :]
    schur = jnp.where(keep, matrix, jnp.float32(0.0))
    panels = jnp.concatenate(collected, axis=1)
    panels = panels.reshape(RB, N_ROW, BLOCK, STEPS * BLOCK).transpose(1, 0, 2, 3).reshape(NT, STEPS * BLOCK)
    return (to_stored(schur), panels)
```

```python
import functools

import jax
import jax.numpy as jnp
from jax import lax
from jax.experimental import pallas as pl
from jax.experimental.pallas import tpu as pltpu
from jax.sharding import PartitionSpec as P

BLOCK = 256
STEPS = 3
EDGE = STEPS * BLOCK
BASE = 128
CHUNK = 128
MESH = pl.DeviceIdType.MESH


def line_width(col_count):
    width = 1
    while 4 * width * width <= col_count:
        width *= 2
    return width


def gather_kernel(row_count, col_count, m_ref, a_ref, r_ref, c_ref, slab_send, slab_recv, edge_send, edge_recv,
                  corner_send, corner_recv, local_sem):
    width = line_width(col_count)
    depth = col_count // width
    rows = m_ref.shape[0]
    chunks = rows // CHUNK
    rounds = chunks // width
    lead = BLOCK // CHUNK
    p = lax.axis_index("row")
    q = lax.axis_index("col")
    a = q // width
    b = q % width

    barrier = pltpu.get_barrier_semaphore()
    for other in range(1, col_count):
        pl.semaphore_signal(barrier, inc=1, device_id=(p, lax.rem(q + other, col_count)), device_id_type=MESH)
    for other in range(1, row_count):
        pl.semaphore_signal(barrier, inc=1, device_id=(lax.rem(p + other, row_count), q), device_id_type=MESH)
    pl.semaphore_wait(barrier, col_count + row_count - 2)

    def slab_copy(k, chunk, way, own, device):
        start = pl.multiple_of(chunk * CHUNK, CHUNK)
        dst = a_ref.at[pl.ds(start, CHUNK), pl.ds(k * BLOCK, BLOCK)]
        src = m_ref.at[pl.ds(start, CHUNK), pl.ds(0, BLOCK)] if own else dst
        return pltpu.make_async_remote_copy(
            src_ref=src,
            dst_ref=dst,
            send_sem=slab_send.at[k, chunk, way],
            recv_sem=slab_recv.at[k, chunk],
            device_id=(p, device),
            device_id_type=MESH,
        )

    def forward(k, chunk, act):
        a0, b0 = k // width, k % width
        part = chunk % width
        mine = part == b

        @pl.when(q == k)
        def _():
            for other in range(width):
                if other != b0:
                    act(slab_copy(k, chunk, 2 + other, True, a0 * width + other))

            @pl.when(mine)
            def _():
                if a0 + 1 < depth:
                    act(slab_copy(k, chunk, 0, True, q + width))
                if a0 > 0:
                    act(slab_copy(k, chunk, 1, True, q - width))

        @pl.when(jnp.logical_and(q != k, mine))
        def _():
            @pl.when(jnp.logical_and(a >= a0, a + 1 < depth))
            def _():
                act(slab_copy(k, chunk, 0, False, q + width))

            @pl.when(jnp.logical_and(a <= a0, a > 0))
            def _():
                act(slab_copy(k, chunk, 1, False, q - width))

            @pl.when(a != a0)
            def _():
                for other in range(1, width):
                    to = lax.rem(b + other, width)
                    act(slab_copy(k, chunk, 2 + to, False, a * width + to))

    def arrive(k, chunk):
        slab_copy(k, chunk, 0, False, q).wait_recv()

    for k in range(STEPS):
        @pl.when(q == k)
        def _():
            pltpu.make_async_copy(
                m_ref.at[:, pl.ds(0, BLOCK)], a_ref.at[:, pl.ds(k * BLOCK, BLOCK)], local_sem.at[0]
            ).start()

            @pl.loop(0, chunks)
            def _(chunk):
                forward(k, chunk, lambda copy: copy.start())

    def relay(step):
        for k in range(STEPS):
            chunk = step * width + b

            @pl.when(q != k)
            def _():
                arrive(k, chunk)
                forward(k, chunk, lambda copy: copy.start())

    def rest(step):
        for k in range(STEPS):
            for other in range(1, width):
                chunk = step * width + lax.rem(b + other, width)

                @pl.when(q != k)
                def _():
                    arrive(k, chunk)

    lead_rounds = -(-lead // width)
    for step in range(lead_rounds):
        relay(jnp.int32(step))
        rest(jnp.int32(step))
    for k in range(STEPS):
        @pl.when(q == k)
        def _():
            pltpu.make_async_copy(
                m_ref.at[:, pl.ds(0, BLOCK)], a_ref.at[:, pl.ds(k * BLOCK, BLOCK)], local_sem.at[0]
            ).wait()

    def corner_copy(i, other):
        return pltpu.make_async_remote_copy(
            src_ref=a_ref.at[pl.ds(0, BLOCK), pl.ds(0, (i + 1) * BLOCK)],
            dst_ref=c_ref.at[pl.ds(i * BLOCK, BLOCK), pl.ds(0, (i + 1) * BLOCK)],
            send_sem=corner_send.at[other],
            recv_sem=corner_recv.at[i],
            device_id=(lax.rem(p + other, row_count), q),
            device_id_type=MESH,
        )

    def edge_copy(i, other):
        return pltpu.make_async_remote_copy(
            src_ref=m_ref.at[pl.ds(0, BLOCK), :],
            dst_ref=r_ref.at[pl.ds(i * BLOCK, BLOCK), :],
            send_sem=edge_send.at[other],
            recv_sem=edge_recv.at[i],
            device_id=(lax.rem(p + other, row_count), q),
            device_id_type=MESH,
        )

    def local_corner(i):
        return pltpu.make_async_copy(
            a_ref.at[pl.ds(0, BLOCK), pl.ds(0, (i + 1) * BLOCK)],
            c_ref.at[pl.ds(i * BLOCK, BLOCK), pl.ds(0, (i + 1) * BLOCK)],
            local_sem.at[1],
        )

    def local_edge(i):
        return pltpu.make_async_copy(
            m_ref.at[pl.ds(0, BLOCK), :], r_ref.at[pl.ds(i * BLOCK, BLOCK), :], local_sem.at[2]
        )

    for i in range(STEPS):
        @pl.when(p == i)
        def _():
            local_corner(i).start()
            local_edge(i).start()
            for other in range(1, row_count):
                corner_copy(i, other).start()
            for other in range(1, row_count):
                edge_copy(i, other).start()

    @pl.loop(lead_rounds, rounds)
    def _(step):
        relay(step)

    @pl.loop(lead_rounds, rounds)
    def _(step):
        rest(step)

    for i in range(STEPS):
        @pl.when(p == i)
        def _():
            local_corner(i).wait()
            local_edge(i).wait()
            for other in range(1, row_count):
                corner_copy(i, other).wait_send()
                edge_copy(i, other).wait_send()

        @pl.when(p != i)
        def _():
            corner_copy(i, 1).wait_recv()
            edge_copy(i, 1).wait_recv()

    for k in range(STEPS):
        @pl.loop(0, chunks)
        def _(chunk):
            forward(k, chunk, lambda copy: copy.wait_send())


def gather(kernel, row_count, col_count):
    rows, cols = kernel.shape
    width = line_width(col_count)
    chunks = rows // CHUNK
    return pl.pallas_call(
        functools.partial(gather_kernel, row_count, col_count),
        out_shape=(
            jax.ShapeDtypeStruct((rows, EDGE), jnp.float32),
            jax.ShapeDtypeStruct((EDGE, cols), jnp.float32),
            jax.ShapeDtypeStruct((EDGE, EDGE), jnp.float32),
        ),
        in_specs=[pl.BlockSpec(memory_space=pl.ANY)],
        out_specs=(pl.BlockSpec(memory_space=pl.ANY),) * 3,
        scratch_shapes=[
            pltpu.SemaphoreType.DMA((STEPS, chunks, 2 + width)),
            pltpu.SemaphoreType.DMA((STEPS, chunks)),
            pltpu.SemaphoreType.DMA((row_count,)),
            pltpu.SemaphoreType.DMA((STEPS,)),
            pltpu.SemaphoreType.DMA((row_count,)),
            pltpu.SemaphoreType.DMA((STEPS,)),
            pltpu.SemaphoreType.DMA((3,)),
        ],
        compiler_params=pltpu.CompilerParams(collective_id=0, has_side_effects=True),
    )(kernel)


def invert_base(block, out_ref):
    tiles = [block[8 * t : 8 * t + 8, :] for t in range(BASE // 8)]
    row_ids = lax.broadcasted_iota(jnp.int32, (8, BASE), 0)
    lane_ids = lax.broadcasted_iota(jnp.int32, (8, BASE), 1)
    aug = [(row_ids + 8 * t == lane_ids).astype(jnp.float32) for t in range(BASE // 8)]

    def row(tile, r):
        return jnp.broadcast_to(tile[r : r + 1, :], (8, BASE))

    for j in range(0, BASE, 2):
        t0, r = j // 8, j % 8
        live = range(t0, BASE // 8)
        first = {t: jnp.broadcast_to(tiles[t][:, j : j + 1], (8, BASE)) for t in live}
        second = {t: jnp.broadcast_to(tiles[t][:, j + 1 : j + 2], (8, BASE)) for t in live}
        d00 = row(first[t0], r)
        d01 = row(second[t0], r)
        d11 = row(second[t0], r + 1)
        i00 = 1.0 / d00
        ratio = d01 * i00
        d11 = d11 - d01 * ratio
        i11 = 1.0 / d11
        a0, a1 = row(tiles[t0], r), row(tiles[t0], r + 1)
        b0, b1 = row(aug[t0], r), row(aug[t0], r + 1)
        a1 = a1 - ratio * a0
        b1 = b1 - ratio * b0
        out_ref[j : j + 1, :] = (b0 * lax.rsqrt(d00))[0:1, :]
        out_ref[j + 1 : j + 2, :] = (b1 * lax.rsqrt(d11))[0:1, :]
        u1 = a1 * i11
        u0 = a0 * i00 - ratio * u1
        v1 = b1 * i11
        v0 = b0 * i00 - ratio * v1
        for t in live:
            tiles[t] = tiles[t] - first[t] * u0 - second[t] * u1
            aug[t] = aug[t] - first[t] * v0 - second[t] * v1


def factor_kernel(c_ref, out_ref, g_ref, w_ref, d_ref):
    for i in range(STEPS):
        rows = slice(i * BLOCK, (i + 1) * BLOCK)
        g_ref[rows, rows] = c_ref[rows, rows]
        for k in range(i):
            cols = slice(k * BLOCK, (k + 1) * BLOCK)
            g_ref[cols, rows] = c_ref[rows, cols].T
            g_ref[rows, cols] = jnp.zeros((BLOCK, BLOCK), jnp.float32)

    @pl.loop(0, EDGE // BASE)
    def _(step):
        here = pl.ds(pl.multiple_of(step * BASE, BASE), BASE)
        invert_base(g_ref[here, here], d_ref)
        inverse = d_ref[...]
        w_ref[...] = jnp.dot(
            inverse, g_ref[here, :], precision=lax.Precision.HIGHEST, preferred_element_type=jnp.float32
        )
        w_ref[:, here] = inverse
        col_ids = lax.broadcasted_iota(jnp.int32, (BASE, EDGE), 1)
        out_ref[here, :] = jnp.where(col_ids < (step + 1) * BASE, w_ref[...], 0.0)

        @pl.loop(step + 1, EDGE // BASE)
        def _(below):
            there = pl.ds(pl.multiple_of(below * BASE, BASE), BASE)
            g_ref[there, here] = jnp.zeros((BASE, BASE), jnp.float32)
            g_ref[there, :] -= jnp.dot(
                w_ref[:, there].T, w_ref[...], precision=lax.Precision.HIGHEST, preferred_element_type=jnp.float32
            )


def factor(corner):
    return pl.pallas_call(
        factor_kernel,
        out_shape=jax.ShapeDtypeStruct((EDGE, EDGE), jnp.float32),
        in_specs=[pl.BlockSpec(memory_space=pltpu.VMEM)],
        out_specs=pl.BlockSpec(memory_space=pltpu.VMEM),
        scratch_shapes=[
            pltpu.VMEM((EDGE, EDGE), jnp.float32),
            pltpu.VMEM((BASE, EDGE), jnp.float32),
            pltpu.VMEM((BASE, BASE), jnp.float32),
        ],
        compiler_params=pltpu.CompilerParams(vmem_limit_bytes=32 * 1024 * 1024),
    )(corner)


def shards(kernel):
    row_count = lax.axis_size("row")
    col_count = lax.axis_size("col")
    row_index = lax.axis_index("row")
    col_index = lax.axis_index("col")
    rows_local, cols_local = kernel.shape
    row_ids = jnp.arange(rows_local) // BLOCK * row_count + row_index
    col_ids = jnp.arange(cols_local) // BLOCK * col_count + col_index
    slabs, edge, corner = gather(kernel, row_count, col_count)
    inverse = factor(corner)
    dot = functools.partial(lax.dot_general, precision=lax.Precision.HIGH, preferred_element_type=jnp.float32)
    panel = dot(slabs, inverse, (((1,), (1,)), ((), ())))
    row_places = row_ids * BLOCK + jnp.arange(rows_local) % BLOCK
    panel = jnp.where(row_places[:, None] >= jnp.arange(EDGE)[None, :], panel, jnp.float32(0.0))
    across = dot(inverse, edge, (((1,), (0,)), ((), ())))
    update = dot(panel, across, (((1,), (0,)), ((), ())))
    keep = (row_ids >= STEPS)[:, None] & (col_ids >= STEPS)[None, :]
    schur = jnp.where(keep, kernel - update, jnp.float32(0.0))
    return (schur, panel)


def solution(mesh):
    return jax.shard_map(
        shards,
        mesh=mesh,
        in_specs=(P("row", "col"),),
        out_specs=(P("row", "col"), P("row", None)),
        check_vma=False,
    )
```

```python
import functools

import jax
import jax.numpy as jnp
from jax import lax
from jax.experimental import pallas as pl
from jax.experimental.pallas import tpu as pltpu
from jax.sharding import PartitionSpec as P

BLOCK = 256
STEPS = 3
EDGE = STEPS * BLOCK
BASE = 128
CHUNK = 128
MESH = pl.DeviceIdType.MESH


def line_width(col_count):
    width = 1
    while 4 * width * width <= col_count:
        width *= 2
    return width


def gather_kernel(row_count, col_count, m_ref, a_ref, r_ref, out_ref, c_ref, g_ref, w_ref, d_ref, slab_send, slab_recv,
                  edge_send, edge_recv, corner_send, corner_recv, local_sem):
    width = line_width(col_count)
    depth = col_count // width
    rows = m_ref.shape[0]
    chunks = rows // CHUNK
    rounds = chunks // width
    lead = BLOCK // CHUNK
    p = lax.axis_index("row")
    q = lax.axis_index("col")
    a = q // width
    b = q % width

    barrier = pltpu.get_barrier_semaphore()
    for other in range(1, col_count):
        pl.semaphore_signal(barrier, inc=1, device_id=(p, lax.rem(q + other, col_count)), device_id_type=MESH)
    for other in range(1, row_count):
        pl.semaphore_signal(barrier, inc=1, device_id=(lax.rem(p + other, row_count), q), device_id_type=MESH)
    pl.semaphore_wait(barrier, col_count + row_count - 2)

    def slab_copy(k, chunk, way, own, device):
        start = pl.multiple_of(chunk * CHUNK, CHUNK)
        dst = a_ref.at[pl.ds(start, CHUNK), pl.ds(k * BLOCK, BLOCK)]
        src = m_ref.at[pl.ds(start, CHUNK), pl.ds(0, BLOCK)] if own else dst
        return pltpu.make_async_remote_copy(
            src_ref=src,
            dst_ref=dst,
            send_sem=slab_send.at[k, chunk, way],
            recv_sem=slab_recv.at[k, chunk],
            device_id=(p, device),
            device_id_type=MESH,
        )

    def forward(k, chunk, act):
        a0, b0 = k // width, k % width
        part = chunk % width
        mine = part == b

        @pl.when(q == k)
        def _():
            for other in range(width):
                if other != b0:
                    act(slab_copy(k, chunk, 2 + other, True, a0 * width + other))

            @pl.when(mine)
            def _():
                if a0 + 1 < depth:
                    act(slab_copy(k, chunk, 0, True, q + width))
                if a0 > 0:
                    act(slab_copy(k, chunk, 1, True, q - width))

        @pl.when(jnp.logical_and(q != k, mine))
        def _():
            @pl.when(jnp.logical_and(a >= a0, a + 1 < depth))
            def _():
                act(slab_copy(k, chunk, 0, False, q + width))

            @pl.when(jnp.logical_and(a <= a0, a > 0))
            def _():
                act(slab_copy(k, chunk, 1, False, q - width))

            @pl.when(a != a0)
            def _():
                for other in range(1, width):
                    to = lax.rem(b + other, width)
                    act(slab_copy(k, chunk, 2 + to, False, a * width + to))

    def arrive(k, chunk):
        slab_copy(k, chunk, 0, False, q).wait_recv()

    for k in range(STEPS):
        @pl.when(q == k)
        def _():
            pltpu.make_async_copy(
                m_ref.at[:, pl.ds(0, BLOCK)], a_ref.at[:, pl.ds(k * BLOCK, BLOCK)], local_sem.at[0]
            ).start()

            @pl.loop(0, chunks)
            def _(chunk):
                forward(k, chunk, lambda copy: copy.start())

    def relay(step):
        for k in range(STEPS):
            chunk = step * width + b

            @pl.when(q != k)
            def _():
                arrive(k, chunk)
                forward(k, chunk, lambda copy: copy.start())

    def rest(step):
        for k in range(STEPS):
            for other in range(1, width):
                chunk = step * width + lax.rem(b + other, width)

                @pl.when(q != k)
                def _():
                    arrive(k, chunk)

    lead_rounds = -(-lead // width)
    for step in range(lead_rounds):
        relay(jnp.int32(step))
        rest(jnp.int32(step))
    for k in range(STEPS):
        @pl.when(q == k)
        def _():
            pltpu.make_async_copy(
                m_ref.at[:, pl.ds(0, BLOCK)], a_ref.at[:, pl.ds(k * BLOCK, BLOCK)], local_sem.at[0]
            ).wait()

    def corner_copy(i, other):
        return pltpu.make_async_remote_copy(
            src_ref=a_ref.at[pl.ds(0, BLOCK), pl.ds(0, (i + 1) * BLOCK)],
            dst_ref=c_ref.at[pl.ds(i * BLOCK, BLOCK), pl.ds(0, (i + 1) * BLOCK)],
            send_sem=corner_send.at[other],
            recv_sem=corner_recv.at[i],
            device_id=(lax.rem(p + other, row_count), q),
            device_id_type=MESH,
        )

    def edge_copy(i, other):
        return pltpu.make_async_remote_copy(
            src_ref=m_ref.at[pl.ds(0, BLOCK), :],
            dst_ref=r_ref.at[pl.ds(i * BLOCK, BLOCK), :],
            send_sem=edge_send.at[other],
            recv_sem=edge_recv.at[i],
            device_id=(lax.rem(p + other, row_count), q),
            device_id_type=MESH,
        )

    def local_corner(i):
        return pltpu.make_async_copy(
            a_ref.at[pl.ds(0, BLOCK), pl.ds(0, (i + 1) * BLOCK)],
            c_ref.at[pl.ds(i * BLOCK, BLOCK), pl.ds(0, (i + 1) * BLOCK)],
            local_sem.at[1],
        )

    def local_edge(i):
        return pltpu.make_async_copy(
            m_ref.at[pl.ds(0, BLOCK), :], r_ref.at[pl.ds(i * BLOCK, BLOCK), :], local_sem.at[2]
        )

    for i in range(STEPS):
        @pl.when(p == i)
        def _():
            local_corner(i).start()
            local_edge(i).start()
            for other in range(1, row_count):
                corner_copy(i, other).start()
            for other in range(1, row_count):
                edge_copy(i, other).start()

    for i in range(STEPS):
        @pl.when(p == i)
        def _():
            local_corner(i).wait()

        @pl.when(p != i)
        def _():
            corner_copy(i, 1).wait_recv()

    def between(step):
        @pl.when(step + lead_rounds < rounds)
        def _():
            relay(step + lead_rounds)

    factor_corner(c_ref, out_ref, g_ref, w_ref, d_ref, between)

    @pl.loop(lead_rounds + EDGE // BASE, rounds)
    def _(step):
        relay(step)

    @pl.loop(lead_rounds, rounds)
    def _(step):
        rest(step)

    for i in range(STEPS):
        @pl.when(p == i)
        def _():
            local_edge(i).wait()
            for other in range(1, row_count):
                corner_copy(i, other).wait_send()
                edge_copy(i, other).wait_send()

        @pl.when(p != i)
        def _():
            edge_copy(i, 1).wait_recv()

    for k in range(STEPS):
        @pl.loop(0, chunks)
        def _(chunk):
            forward(k, chunk, lambda copy: copy.wait_send())


def gather(kernel, row_count, col_count):
    rows, cols = kernel.shape
    width = line_width(col_count)
    chunks = rows // CHUNK
    return pl.pallas_call(
        functools.partial(gather_kernel, row_count, col_count),
        out_shape=(
            jax.ShapeDtypeStruct((rows, EDGE), jnp.float32),
            jax.ShapeDtypeStruct((EDGE, cols), jnp.float32),
            jax.ShapeDtypeStruct((EDGE, EDGE), jnp.float32),
        ),
        in_specs=[pl.BlockSpec(memory_space=pl.ANY)],
        out_specs=(
            pl.BlockSpec(memory_space=pl.ANY),
            pl.BlockSpec(memory_space=pl.ANY),
            pl.BlockSpec(memory_space=pltpu.VMEM),
        ),
        scratch_shapes=[
            pltpu.VMEM((EDGE, EDGE), jnp.float32),
            pltpu.VMEM((EDGE, EDGE), jnp.float32),
            pltpu.VMEM((BASE, EDGE), jnp.float32),
            pltpu.VMEM((BASE, BASE), jnp.float32),
            pltpu.SemaphoreType.DMA((STEPS, chunks, 2 + width)),
            pltpu.SemaphoreType.DMA((STEPS, chunks)),
            pltpu.SemaphoreType.DMA((row_count,)),
            pltpu.SemaphoreType.DMA((STEPS,)),
            pltpu.SemaphoreType.DMA((row_count,)),
            pltpu.SemaphoreType.DMA((STEPS,)),
            pltpu.SemaphoreType.DMA((3,)),
        ],
        compiler_params=pltpu.CompilerParams(
            collective_id=0, has_side_effects=True, vmem_limit_bytes=32 * 1024 * 1024
        ),
    )(kernel)


def invert_base(block, out_ref):
    tiles = [block[8 * t : 8 * t + 8, :] for t in range(BASE // 8)]
    row_ids = lax.broadcasted_iota(jnp.int32, (8, BASE), 0)
    lane_ids = lax.broadcasted_iota(jnp.int32, (8, BASE), 1)
    aug = [(row_ids + 8 * t == lane_ids).astype(jnp.float32) for t in range(BASE // 8)]

    def row(tile, r):
        return jnp.broadcast_to(tile[r : r + 1, :], (8, BASE))

    for j in range(0, BASE, 2):
        t0, r = j // 8, j % 8
        live = range(t0, BASE // 8)
        first = {t: jnp.broadcast_to(tiles[t][:, j : j + 1], (8, BASE)) for t in live}
        second = {t: jnp.broadcast_to(tiles[t][:, j + 1 : j + 2], (8, BASE)) for t in live}
        d00 = row(first[t0], r)
        d01 = row(second[t0], r)
        d11 = row(second[t0], r + 1)
        i00 = 1.0 / d00
        ratio = d01 * i00
        d11 = d11 - d01 * ratio
        i11 = 1.0 / d11
        a0, a1 = row(tiles[t0], r), row(tiles[t0], r + 1)
        b0, b1 = row(aug[t0], r), row(aug[t0], r + 1)
        a1 = a1 - ratio * a0
        b1 = b1 - ratio * b0
        out_ref[j : j + 1, :] = (b0 * lax.rsqrt(d00))[0:1, :]
        out_ref[j + 1 : j + 2, :] = (b1 * lax.rsqrt(d11))[0:1, :]
        u1 = a1 * i11
        u0 = a0 * i00 - ratio * u1
        v1 = b1 * i11
        v0 = b0 * i00 - ratio * v1
        for t in live:
            tiles[t] = tiles[t] - first[t] * u0 - second[t] * u1
            aug[t] = aug[t] - first[t] * v0 - second[t] * v1


def factor_corner(c_ref, out_ref, g_ref, w_ref, d_ref, between):
    for i in range(STEPS):
        rows = slice(i * BLOCK, (i + 1) * BLOCK)
        g_ref[rows, rows] = c_ref[rows, rows]
        for k in range(i):
            cols = slice(k * BLOCK, (k + 1) * BLOCK)
            g_ref[cols, rows] = c_ref[rows, cols].T
            g_ref[rows, cols] = jnp.zeros((BLOCK, BLOCK), jnp.float32)

    @pl.loop(0, EDGE // BASE)
    def _(step):
        between(step)
        here = pl.ds(pl.multiple_of(step * BASE, BASE), BASE)
        invert_base(g_ref[here, here], d_ref)
        inverse = d_ref[...]
        w_ref[...] = jnp.dot(
            inverse, g_ref[here, :], precision=lax.Precision.HIGHEST, preferred_element_type=jnp.float32
        )
        w_ref[:, here] = inverse
        col_ids = lax.broadcasted_iota(jnp.int32, (BASE, EDGE), 1)
        out_ref[here, :] = jnp.where(col_ids < (step + 1) * BASE, w_ref[...], 0.0)

        @pl.loop(step + 1, EDGE // BASE)
        def _(below):
            there = pl.ds(pl.multiple_of(below * BASE, BASE), BASE)
            g_ref[there, here] = jnp.zeros((BASE, BASE), jnp.float32)
            g_ref[there, :] -= jnp.dot(
                w_ref[:, there].T, w_ref[...], precision=lax.Precision.HIGHEST, preferred_element_type=jnp.float32
            )


def shards(kernel):
    row_count = lax.axis_size("row")
    col_count = lax.axis_size("col")
    row_index = lax.axis_index("row")
    col_index = lax.axis_index("col")
    rows_local, cols_local = kernel.shape
    row_ids = jnp.arange(rows_local) // BLOCK * row_count + row_index
    col_ids = jnp.arange(cols_local) // BLOCK * col_count + col_index
    slabs, edge, inverse = gather(kernel, row_count, col_count)
    dot = functools.partial(lax.dot_general, precision=lax.Precision.HIGH, preferred_element_type=jnp.float32)
    panel = dot(slabs, inverse, (((1,), (1,)), ((), ())))
    row_places = row_ids * BLOCK + jnp.arange(rows_local) % BLOCK
    panel = jnp.where(row_places[:, None] >= jnp.arange(EDGE)[None, :], panel, jnp.float32(0.0))
    across = dot(inverse, edge, (((1,), (0,)), ((), ())))
    update = dot(panel, across, (((1,), (0,)), ((), ())))
    keep = (row_ids >= STEPS)[:, None] & (col_ids >= STEPS)[None, :]
    schur = jnp.where(keep, kernel - update, jnp.float32(0.0))
    return (schur, panel)


def solution(mesh):
    return jax.shard_map(
        shards,
        mesh=mesh,
        in_specs=(P("row", "col"),),
        out_specs=(P("row", "col"), P("row", None)),
        check_vma=False,
    )
```

```python
import functools

import jax
import jax.numpy as jnp
from jax import lax
from jax.experimental import pallas as pl
from jax.experimental.pallas import tpu as pltpu
from jax.sharding import PartitionSpec as P

BLOCK = 256
STEPS = 3
EDGE = STEPS * BLOCK
BASE = 128
CHUNK = 128
MESH = pl.DeviceIdType.MESH


def line_width(col_count):
    width = 1
    while 4 * width * width <= col_count:
        width *= 2
    return width


def gather_kernel(row_count, col_count, m_ref, a_ref, r_ref, out_ref, c_ref, g_ref, w_ref, d_ref, slab_send, slab_recv,
                  edge_send, edge_recv, corner_send, corner_recv, local_sem):
    width = line_width(col_count)
    depth = col_count // width
    rows = m_ref.shape[0]
    chunks = rows // CHUNK
    rounds = chunks // width
    lead = BLOCK // CHUNK
    p = lax.axis_index("row")
    q = lax.axis_index("col")
    a = q // width
    b = q % width

    barrier = pltpu.get_barrier_semaphore()
    for other in range(1, col_count):
        pl.semaphore_signal(barrier, inc=1, device_id=(p, lax.rem(q + other, col_count)), device_id_type=MESH)
    for other in range(1, row_count):
        pl.semaphore_signal(barrier, inc=1, device_id=(lax.rem(p + other, row_count), q), device_id_type=MESH)
    pl.semaphore_wait(barrier, col_count + row_count - 2)

    def slab_copy(k, chunk, way, own, device):
        start = pl.multiple_of(chunk * CHUNK, CHUNK)
        dst = a_ref.at[pl.ds(start, CHUNK), pl.ds(k * BLOCK, BLOCK)]
        src = m_ref.at[pl.ds(start, CHUNK), pl.ds(0, BLOCK)] if own else dst
        return pltpu.make_async_remote_copy(
            src_ref=src,
            dst_ref=dst,
            send_sem=slab_send.at[k, chunk, way],
            recv_sem=slab_recv.at[k, chunk],
            device_id=(p, device),
            device_id_type=MESH,
        )

    def forward(k, chunk, act):
        a0, b0 = k // width, k % width
        part = chunk % width
        mine = part == b

        @pl.when(q == k)
        def _():
            for other in range(width):
                if other != b0:
                    act(slab_copy(k, chunk, 2 + other, True, a0 * width + other))

            @pl.when(mine)
            def _():
                if a0 + 1 < depth:
                    act(slab_copy(k, chunk, 0, True, q + width))
                if a0 > 0:
                    act(slab_copy(k, chunk, 1, True, q - width))

        @pl.when(jnp.logical_and(q != k, mine))
        def _():
            @pl.when(jnp.logical_and(a >= a0, a + 1 < depth))
            def _():
                act(slab_copy(k, chunk, 0, False, q + width))

            @pl.when(jnp.logical_and(a <= a0, a > 0))
            def _():
                act(slab_copy(k, chunk, 1, False, q - width))

            @pl.when(a != a0)
            def _():
                for other in range(1, width):
                    to = lax.rem(b + other, width)
                    act(slab_copy(k, chunk, 2 + to, False, a * width + to))

    def arrive(k, chunk):
        slab_copy(k, chunk, 0, False, q).wait_recv()

    for k in range(STEPS):
        @pl.when(q == k)
        def _():
            pltpu.make_async_copy(
                m_ref.at[:, pl.ds(0, BLOCK)], a_ref.at[:, pl.ds(k * BLOCK, BLOCK)], local_sem.at[0]
            ).start()

    def relay(step):
        for k in range(STEPS):
            @pl.when(q == k)
            def _():
                for part in range(width):
                    forward(k, step * width + part, lambda copy: copy.start())

        for k in range(STEPS):
            chunk = step * width + b

            @pl.when(q != k)
            def _():
                arrive(k, chunk)
                forward(k, chunk, lambda copy: copy.start())

    def rest(step):
        for k in range(STEPS):
            for other in range(1, width):
                chunk = step * width + lax.rem(b + other, width)

                @pl.when(q != k)
                def _():
                    arrive(k, chunk)

    lead_rounds = -(-lead // width)
    for step in range(lead_rounds):
        relay(jnp.int32(step))
        rest(jnp.int32(step))
    for k in range(STEPS):
        @pl.when(q == k)
        def _():
            pltpu.make_async_copy(
                m_ref.at[:, pl.ds(0, BLOCK)], a_ref.at[:, pl.ds(k * BLOCK, BLOCK)], local_sem.at[0]
            ).wait()

    def corner_copy(i, other):
        return pltpu.make_async_remote_copy(
            src_ref=a_ref.at[pl.ds(0, BLOCK), pl.ds(0, (i + 1) * BLOCK)],
            dst_ref=c_ref.at[pl.ds(i * BLOCK, BLOCK), pl.ds(0, (i + 1) * BLOCK)],
            send_sem=corner_send.at[other],
            recv_sem=corner_recv.at[i],
            device_id=(lax.rem(p + other, row_count), q),
            device_id_type=MESH,
        )

    def edge_copy(i, other, piece):
        start = pl.multiple_of(piece * (BLOCK // rounds), BLOCK // rounds)
        return pltpu.make_async_remote_copy(
            src_ref=m_ref.at[pl.ds(start, BLOCK // rounds), :],
            dst_ref=r_ref.at[pl.ds(i * BLOCK + start, BLOCK // rounds), :],
            send_sem=edge_send.at[other, piece],
            recv_sem=edge_recv.at[i, piece],
            device_id=(lax.rem(p + other, row_count), q),
            device_id_type=MESH,
        )

    def edge_round(piece):
        for i in range(STEPS):
            @pl.when(p == i)
            def _():
                for other in range(1, row_count):
                    edge_copy(i, other, piece).start()

    def local_corner(i):
        return pltpu.make_async_copy(
            a_ref.at[pl.ds(0, BLOCK), pl.ds(0, (i + 1) * BLOCK)],
            c_ref.at[pl.ds(i * BLOCK, BLOCK), pl.ds(0, (i + 1) * BLOCK)],
            local_sem.at[1],
        )

    def local_edge(i):
        return pltpu.make_async_copy(
            m_ref.at[pl.ds(0, BLOCK), :], r_ref.at[pl.ds(i * BLOCK, BLOCK), :], local_sem.at[2]
        )

    for i in range(STEPS):
        @pl.when(p == i)
        def _():
            local_corner(i).start()
            local_edge(i).start()
            for other in range(1, row_count):
                corner_copy(i, other).start()

    for step in range(lead_rounds):
        edge_round(jnp.int32(step))

    for i in range(STEPS):
        @pl.when(p == i)
        def _():
            local_corner(i).wait()

        @pl.when(p != i)
        def _():
            corner_copy(i, 1).wait_recv()

    def between(step):
        @pl.when(step + lead_rounds < rounds)
        def _():
            relay(step + lead_rounds)
            edge_round(step + lead_rounds)

    factor_corner(c_ref, out_ref, g_ref, w_ref, d_ref, between)

    @pl.loop(lead_rounds + EDGE // BASE, rounds)
    def _(step):
        relay(step)
        edge_round(step)

    @pl.loop(lead_rounds, rounds)
    def _(step):
        rest(step)

    for i in range(STEPS):
        @pl.when(p == i)
        def _():
            local_edge(i).wait()
            for other in range(1, row_count):
                corner_copy(i, other).wait_send()

            @pl.loop(0, rounds)
            def _(piece):
                for other in range(1, row_count):
                    edge_copy(i, other, piece).wait_send()

        @pl.when(p != i)
        def _():
            @pl.loop(0, rounds)
            def _(piece):
                edge_copy(i, 1, piece).wait_recv()

    for k in range(STEPS):
        @pl.loop(0, chunks)
        def _(chunk):
            forward(k, chunk, lambda copy: copy.wait_send())


def gather(kernel, row_count, col_count):
    rows, cols = kernel.shape
    width = line_width(col_count)
    chunks = rows // CHUNK
    return pl.pallas_call(
        functools.partial(gather_kernel, row_count, col_count),
        out_shape=(
            jax.ShapeDtypeStruct((rows, EDGE), jnp.float32),
            jax.ShapeDtypeStruct((EDGE, cols), jnp.float32),
            jax.ShapeDtypeStruct((EDGE, EDGE), jnp.float32),
        ),
        in_specs=[pl.BlockSpec(memory_space=pl.ANY)],
        out_specs=(
            pl.BlockSpec(memory_space=pl.ANY),
            pl.BlockSpec(memory_space=pl.ANY),
            pl.BlockSpec(memory_space=pltpu.VMEM),
        ),
        scratch_shapes=[
            pltpu.VMEM((EDGE, EDGE), jnp.float32),
            pltpu.VMEM((EDGE, EDGE), jnp.float32),
            pltpu.VMEM((BASE, EDGE), jnp.float32),
            pltpu.VMEM((BASE, BASE), jnp.float32),
            pltpu.SemaphoreType.DMA((STEPS, chunks, 2 + width)),
            pltpu.SemaphoreType.DMA((STEPS, chunks)),
            pltpu.SemaphoreType.DMA((row_count, chunks // width)),
            pltpu.SemaphoreType.DMA((STEPS, chunks // width)),
            pltpu.SemaphoreType.DMA((row_count,)),
            pltpu.SemaphoreType.DMA((STEPS,)),
            pltpu.SemaphoreType.DMA((3,)),
        ],
        compiler_params=pltpu.CompilerParams(
            collective_id=0, has_side_effects=True, vmem_limit_bytes=32 * 1024 * 1024
        ),
    )(kernel)


def invert_base(block, out_ref):
    tiles = [block[8 * t : 8 * t + 8, :] for t in range(BASE // 8)]
    row_ids = lax.broadcasted_iota(jnp.int32, (8, BASE), 0)
    lane_ids = lax.broadcasted_iota(jnp.int32, (8, BASE), 1)
    aug = [(row_ids + 8 * t == lane_ids).astype(jnp.float32) for t in range(BASE // 8)]

    def row(tile, r):
        return jnp.broadcast_to(tile[r : r + 1, :], (8, BASE))

    for j in range(0, BASE, 2):
        t0, r = j // 8, j % 8
        live = range(t0, BASE // 8)
        first = {t: jnp.broadcast_to(tiles[t][:, j : j + 1], (8, BASE)) for t in live}
        second = {t: jnp.broadcast_to(tiles[t][:, j + 1 : j + 2], (8, BASE)) for t in live}
        d00 = row(first[t0], r)
        d01 = row(second[t0], r)
        d11 = row(second[t0], r + 1)
        i00 = 1.0 / d00
        ratio = d01 * i00
        d11 = d11 - d01 * ratio
        i11 = 1.0 / d11
        a0, a1 = row(tiles[t0], r), row(tiles[t0], r + 1)
        b0, b1 = row(aug[t0], r), row(aug[t0], r + 1)
        a1 = a1 - ratio * a0
        b1 = b1 - ratio * b0
        out_ref[j : j + 1, :] = (b0 * lax.rsqrt(d00))[0:1, :]
        out_ref[j + 1 : j + 2, :] = (b1 * lax.rsqrt(d11))[0:1, :]
        u1 = a1 * i11
        u0 = a0 * i00 - ratio * u1
        v1 = b1 * i11
        v0 = b0 * i00 - ratio * v1
        for t in live:
            tiles[t] = tiles[t] - first[t] * u0 - second[t] * u1
            aug[t] = aug[t] - first[t] * v0 - second[t] * v1


def factor_corner(c_ref, out_ref, g_ref, w_ref, d_ref, between):
    for i in range(STEPS):
        rows = slice(i * BLOCK, (i + 1) * BLOCK)
        g_ref[rows, rows] = c_ref[rows, rows]
        for k in range(i):
            cols = slice(k * BLOCK, (k + 1) * BLOCK)
            g_ref[cols, rows] = c_ref[rows, cols].T
            g_ref[rows, cols] = jnp.zeros((BLOCK, BLOCK), jnp.float32)

    @pl.loop(0, EDGE // BASE)
    def _(step):
        between(step)
        here = pl.ds(pl.multiple_of(step * BASE, BASE), BASE)
        invert_base(g_ref[here, here], d_ref)
        inverse = d_ref[...]
        w_ref[...] = jnp.dot(
            inverse, g_ref[here, :], precision=lax.Precision.HIGHEST, preferred_element_type=jnp.float32
        )
        w_ref[:, here] = inverse
        col_ids = lax.broadcasted_iota(jnp.int32, (BASE, EDGE), 1)
        out_ref[here, :] = jnp.where(col_ids < (step + 1) * BASE, w_ref[...], 0.0)

        @pl.loop(step + 1, EDGE // BASE)
        def _(below):
            there = pl.ds(pl.multiple_of(below * BASE, BASE), BASE)
            g_ref[there, here] = jnp.zeros((BASE, BASE), jnp.float32)
            g_ref[there, :] -= jnp.dot(
                w_ref[:, there].T, w_ref[...], precision=lax.Precision.HIGHEST, preferred_element_type=jnp.float32
            )


def shards(kernel):
    row_count = lax.axis_size("row")
    col_count = lax.axis_size("col")
    row_index = lax.axis_index("row")
    col_index = lax.axis_index("col")
    rows_local, cols_local = kernel.shape
    row_ids = jnp.arange(rows_local) // BLOCK * row_count + row_index
    col_ids = jnp.arange(cols_local) // BLOCK * col_count + col_index
    slabs, edge, inverse = gather(kernel, row_count, col_count)
    dot = functools.partial(lax.dot_general, precision=lax.Precision.HIGH, preferred_element_type=jnp.float32)
    panel = dot(slabs, inverse, (((1,), (1,)), ((), ())))
    row_places = row_ids * BLOCK + jnp.arange(rows_local) % BLOCK
    panel = jnp.where(row_places[:, None] >= jnp.arange(EDGE)[None, :], panel, jnp.float32(0.0))
    across = dot(inverse, edge, (((1,), (0,)), ((), ())))
    update = dot(panel, across, (((1,), (0,)), ((), ())))
    keep = (row_ids >= STEPS)[:, None] & (col_ids >= STEPS)[None, :]
    schur = jnp.where(keep, kernel - update, jnp.float32(0.0))
    return (schur, panel)


def solution(mesh):
    return jax.shard_map(
        shards,
        mesh=mesh,
        in_specs=(P("row", "col"),),
        out_specs=(P("row", "col"), P("row", None)),
        check_vma=False,
    )
```
